32 devices in a mesh: hid: 8 (over z, x), ffn: 4 (over y, core).
Axes of the slice: x: 2, y: 2, z: 4, core: 2. Of those that a mesh axis runs over, the one named last changes fastest.
Arguments:
- tokens: bfloat16 [256, 8192], P('ffn', 'hid'), may hold values from -128 to 128
- lang_ids: int32 [256], P('ffn'), may hold values from 0 to 15
- gain_table: float32 [16, 8192], P(None, 'hid'), may hold values from 0.1 to 1.9
- gate_weight: bfloat16 [8192, 28672], P('hid', 'ffn'), may hold values from -0.0625 to 0.0625
- up_weight: bfloat16 [8192, 28672], P('hid', 'ffn'), may hold values from -0.0625 to 0.0625
- down_weight: bfloat16 [28672, 8192], P('ffn', 'hid'), may hold values from -0.03125 to 0.03125
Outputs:
- mixed: bfloat16 [256, 8192], P('ffn', 'hid')
The draws below stay inside these ranges and needn't reach their ends.
All inputs are finite; a program needn't handle non-finite values.
Results may differ from the reference program's by a relative error of at most 0.012.
Values may be sent and summed in bfloat16 or wider, within the bound.
A program may use at most 128 MiB of HBM per device.

```python
import math
import jax
import jax.numpy as jnp
from jax import lax

D = 8192
FF = 28672
LANGS = 16
TOKENS = 256
N_HID = 8


def draw_tokens(key, part):
    key = jax.random.fold_in(key, 7)
    key_base, key_cols, key_rows = jax.random.split(key, 3)
    column_scale = 0.6 * 3.0 ** (jnp.arange(D, dtype=jnp.float32) / D)
    column_scale = column_scale * jnp.exp(jax.random.uniform(key_cols, (D,), jnp.float32, -0.35, 0.35))
    base = jnp.clip(jax.random.normal(key_base, (TOKENS, D), jnp.float32), -5.0, 5.0)
    row_scale = jnp.exp(jax.random.uniform(key_rows, (TOKENS, 1), jnp.float32, 0.0, math.log(10.0)))
    return (base * row_scale * column_scale[None, :]).astype(jnp.bfloat16)


def plant(array, own_key, smallest, largest):
    longest = array.shape.index(max(array.shape))
    spots = []
    for shift in (0, 1):
        where = [jax.random.randint(jax.random.fold_in(own_key, axis), (), 0, length) for axis, length in enumerate(array.shape)]
        where[longest] = (where[longest] + shift) % array.shape[longest]
        spots.append(tuple(where))
    return array.at[spots[0]].set(smallest).at[spots[1]].set(largest)


def steps_of(key, extent, cuts, smallest, high):
    factor_of, own = 1.0, jax.random.fold_in(key, 6)
    for axis_at, blocks in cuts:
        draws = jnp.exp(jax.random.uniform(jax.random.fold_in(own, axis_at), (blocks,), jnp.float32, smallest / len(cuts), high / len(cuts)))
        factor_of = factor_of * jnp.repeat(draws, extent[axis_at] // blocks).reshape([-1 if axis == axis_at else 1 for axis in range(len(extent))])
    return factor_of


def gaussian(own_key, shape, spread, reach, cuts=(), kind=jnp.bfloat16):
    level = steps_of(own_key, shape, cuts, -0.22, 0.18) if cuts else 1.0
    array = jax.random.normal(own_key, shape, jnp.float32) * spread * level
    return jnp.minimum(jnp.maximum(array, -reach), reach).astype(kind)


def setup_inputs(seed: int = 0) -> dict:
    splits = jax.random.split(jax.random.key(seed), 7)
    tokens = draw_tokens(jax.random.fold_in(splits[6], 71), 0)
    lang_ids = plant(jax.random.randint(splits[1], (TOKENS,), 0, LANGS), jax.random.fold_in(splits[1], 1), 0, LANGS - 1).astype(jnp.int32)
    gain_table = jnp.clip(1.0 + 0.18 * jax.random.normal(splits[2], (LANGS, D), jnp.float32), 0.1, 1.9)
    gate_weight = gaussian(splits[3], (D, FF), D ** -0.5, 0.0625, ((0, 8), (1, 4)))
    up_weight = gaussian(splits[4], (D, FF), D ** -0.5, 0.0625, ((0, 8), (1, 4)))
    down_weight = gaussian(splits[5], (FF, D), FF ** -0.5, 0.03125, ((0, 4), (1, 8)))
    return {"tokens": tokens, "lang_ids": lang_ids, "gain_table": gain_table, "gate_weight": gate_weight, "up_weight": up_weight, "down_weight": down_weight}


def reference(tokens, lang_ids, gain_table, gate_weight, up_weight, down_weight):
    values = tokens.astype(jnp.float32)
    inverse_rms = lax.rsqrt(lax.optimization_barrier(jnp.mean(values * values, axis=1)) + 1e-05)
    scaled = (values * gain_table[lang_ids]).astype(jnp.bfloat16)
    block_width = D // N_HID
    blocks_in = scaled.reshape(TOKENS, N_HID, block_width).transpose(1, 0, 2)
    both_weights = jnp.concatenate([gate_weight, up_weight], axis=1)
    blocks_weight = both_weights.reshape(N_HID, block_width, 2 * FF)

    def accumulate(total, pair):
        partial_term = jnp.dot(pair[0], pair[1], preferred_element_type=jnp.float32).astype(jnp.bfloat16)
        partial_term = lax.optimization_barrier(partial_term)
        return (total + partial_term.astype(jnp.float32), None)
    summed, _ = lax.scan(accumulate, jnp.zeros((TOKENS, 2 * FF), jnp.float32), (blocks_in, blocks_weight))
    gate_sum = summed[:, :FF] * inverse_rms[:, None]
    up_sum = summed[:, FF:] * inverse_rms[:, None]
    hidden = (jax.nn.silu(gate_sum) * up_sum).astype(jnp.bfloat16)
    projected = jnp.dot(hidden, down_weight, preferred_element_type=jnp.float32)
    return (values + projected).astype(jnp.bfloat16)
```

```python
import functools

import jax
import jax.numpy as jnp
from jax import lax
from jax.experimental import pallas as pl
from jax.experimental.pallas import tpu as pltpu
from jax.sharding import PartitionSpec as P

BF16, F32 = jnp.bfloat16, jnp.float32
PIECES = 4
TILE = 256


def gather_then_sum(tokens, lang_ids, gain_table, gate_weight, up_weight, down_weight):
    hid_count = lax.axis_size("hid")
    unit_count = gate_weight.shape[1]
    feature_total = tokens.shape[1] * hid_count
    one_hot = (
        lang_ids[:, None] == jnp.arange(gain_table.shape[0], dtype=jnp.int32)[None, :]
    ).astype(F32)
    token_gains = jnp.dot(one_hot, gain_table, precision=lax.Precision.HIGHEST)
    values = tokens.astype(F32)
    scaled = (values * token_gains).astype(BF16)
    squares = jnp.sum(values * values, axis=1)
    square_pieces = lax.all_gather(squares, "ffn", axis=0, tiled=True)
    all_squares = lax.psum(square_pieces, "hid")
    inverse_rms = lax.rsqrt(all_squares / feature_total + 1e-05)
    both_weights = jnp.concatenate([gate_weight, up_weight], axis=1)
    gathered = lax.all_gather(scaled, "ffn", axis=0, tiled=True)
    partial_sums = jnp.dot(gathered, both_weights, preferred_element_type=F32)
    summed = lax.psum(partial_sums.astype(BF16), "hid").astype(F32)
    gate_sum = summed[:, :unit_count] * inverse_rms[:, None]
    up_sum = summed[:, unit_count:] * inverse_rms[:, None]
    hidden = (jax.nn.silu(gate_sum) * up_sum).astype(BF16)
    down_terms = jnp.dot(hidden, down_weight, preferred_element_type=F32)
    own_rows = lax.psum_scatter(
        down_terms.astype(BF16), "ffn", scatter_dimension=0, tiled=True
    ).astype(F32)
    return (values + own_rows).astype(BF16)


def kernel(
    n, m, tokens_ref, ids_ref, gain_ref, gate_ref, up_ref, down_ref, out_ref,
    xall, wbuf, part, recv, hidden, down, acc, rowinv, squares, inverse, yout, yin,
    xs_sem, xr_sem, w_sem, d_sem, rs_sem, rr_sem, gs_sem, gr_sem,
    qs_sem, qr_sem, is_sem, ir_sem, ys_sem, yr_sem,
):
    h = lax.axis_index("hid")
    f = lax.axis_index("ffn")
    rows, features = tokens_ref.shape
    units = hidden.shape[2]
    half = n // 2
    side = rows * m // 2
    piece = side // PIECES

    odd = lax.rem(h, 2)
    p = (1 - odd) * (h // 2) + odd * (n - (h + 1) // 2)

    def hid_at(q):
        back = q // half
        return (1 - back) * 2 * q + back * (2 * n - 1 - 2 * q)

    right = hid_at(lax.rem(p + 1, n))
    left = hid_at(lax.rem(p + n - 1, n))
    towards = (right, left)

    def weight_copies(s, b):
        offset = n - 1 - s if b == 0 else lax.rem(s + 1, half)
        chunk = lax.rem(p + offset, n)
        slot = 2 * lax.rem(s, 2) + b
        columns = pl.ds(pl.multiple_of(chunk * units, 128), units)
        return [
            pltpu.make_async_copy(
                ref.at[:, columns], wbuf.at[slot, :, pl.ds(i * units, units)], w_sem.at[slot, i]
            )
            for i, ref in enumerate((gate_ref, up_ref))
        ]

    def start_weights(s):
        for b in range(2):
            for copy in weight_copies(s, b):
                copy.start()

    start_weights(0)
    start_weights(1)

    barrier = pltpu.get_barrier_semaphore()
    for i in range(1, n):
        pl.semaphore_signal(barrier, inc=1, device_id={"hid": lax.rem(h + i, n)})
    for i in range(1, m):
        pl.semaphore_signal(barrier, inc=1, device_id={"ffn": lax.rem(f + i, m)})

    values = tokens_ref[...].astype(F32)
    ids = ids_ref[...]
    gains = jnp.zeros((rows, features), F32)
    for lang in range(gain_ref.shape[0]):
        gains = jnp.where(ids == lang, gain_ref[lang : lang + 1, :], gains)
    own_rows = pl.ds(pl.multiple_of(f * rows, rows), rows)
    xall[own_rows, :] = (values * gains).astype(BF16)
    diagonal = lax.broadcasted_iota(jnp.int32, (rows, 128), 0) == lax.broadcasted_iota(
        jnp.int32, (rows, 128), 1
    )
    sums = jnp.sum(values * values, axis=1, keepdims=True)
    in_lanes = jnp.sum(jnp.where(diagonal, sums, 0.0), axis=0, keepdims=True)
    squares[0] = jnp.broadcast_to(in_lanes, (8, 128))

    pl.semaphore_wait(barrier, n - 1 + m - 1)

    def x_copy(i, sender):
        block = xall.at[pl.ds(pl.multiple_of(sender * rows, rows), rows), :]
        return pltpu.make_async_remote_copy(
            src_ref=block, dst_ref=block, send_sem=xs_sem.at[i], recv_sem=xr_sem.at[i],
            device_id={"ffn": lax.rem(f + i, m)},
        )

    def square_copy(i):
        return pltpu.make_async_remote_copy(
            src_ref=squares.at[0], dst_ref=squares.at[i],
            send_sem=qs_sem.at[i], recv_sem=qr_sem.at[i],
            device_id={"hid": lax.rem(h + i, n)},
        )

    def inverse_copy(i, sender):
        return pltpu.make_async_remote_copy(
            src_ref=inverse.at[sender], dst_ref=inverse.at[sender],
            send_sem=is_sem.at[i], recv_sem=ir_sem.at[i],
            device_id={"ffn": lax.rem(f + i, m)},
        )

    for i in range(1, m):
        x_copy(i, f).start()
    for i in range(1, n):
        square_copy(i).start()
    for i in range(1, m):
        x_copy(i, lax.rem(f + m - i, m)).wait_recv()

    def project(s, b):
        offset = n - 1 - s if b == 0 else lax.rem(s + 1, half)
        chunk = lax.rem(p + offset, n)
        slot = 2 * lax.rem(s, 2) + b
        for copy in weight_copies(s, b):
            copy.wait()

        def tile(t, _):
            columns = pl.ds(pl.multiple_of(t * TILE, TILE), TILE)
            part[chunk, :, columns] = jnp.dot(
                xall[...], wbuf[slot, :, columns], preferred_element_type=F32
            ).astype(BF16)
            return 0

        lax.fori_loop(0, 2 * units // TILE, tile, 0)

    def sum_copy(s, d, q):
        chunk = lax.rem(p + n - 1 - s, n) if d == 0 else lax.rem(p + 1 + s, n)
        return chunk, pltpu.make_async_remote_copy(
            src_ref=part.at[chunk, pl.ds(d * side + q * piece, piece), :],
            dst_ref=recv.at[d, s, pl.ds(q * piece, piece), :],
            send_sem=rs_sem.at[d, s, q], recv_sem=rr_sem.at[d, s, q],
            device_id={"hid": towards[d]},
        )

    def pass_sums(s):
        for q in range(PIECES):
            for d in range(2):
                chunk, copy = sum_copy(s, d, q)
                sum_copy(s - 1, d, q)[1].wait_recv()
                here = pl.ds(d * side + q * piece, piece)
                part[chunk, here, :] = (
                    part[chunk, here, :].astype(F32)
                    + recv[d, s - 1, pl.ds(q * piece, piece), :].astype(F32)
                ).astype(BF16)
                copy.start()

    for d in range(2):
        project(0, d)
        for q in range(PIECES):
            sum_copy(0, d, q)[1].start()
    start_weights(2)

    def early(s, _):
        project(s, 0)
        project(s, 1)

        @pl.when(s + 2 < half)
        def _():
            start_weights(s + 2)

        pass_sums(s)
        return 0

    lax.fori_loop(1, half, early, 0)

    def down_copy(c):
        block = pl.ds(c * units, units)
        return pltpu.make_async_copy(down_ref.at[block, :], down.at[block, :], d_sem.at[c])

    for c in range(n):
        down_copy(c).start()

    for i in range(1, n):
        square_copy(i).wait_recv()
    total = squares[0]
    for i in range(1, n):
        total = total + squares[i]
    inverse[f] = lax.rsqrt(total / (features * n) + 1e-05)
    for i in range(1, m):
        inverse_copy(i, f).start()

    def late(s, _):
        pass_sums(s)
        return 0

    lax.fori_loop(half, n - 1, late, 0)

    for i in range(1, m):
        inverse_copy(i, lax.rem(f + m - i, m)).wait_recv()
    for j in range(m):
        column = jnp.sum(
            jnp.where(diagonal, inverse[j, 0:1, :], 0.0), axis=1, keepdims=True
        )
        rowinv[j * rows : (j + 1) * rows, :] = jnp.broadcast_to(column, (rows, 128))

    def hidden_copy(s, d, q):
        chunk = lax.rem(p + n - s, n) if d == 0 else lax.rem(p + s, n)
        block = hidden.at[chunk, pl.ds(d * side + q * piece, piece), :]
        return pltpu.make_async_remote_copy(
            src_ref=block, dst_ref=block,
            send_sem=gs_sem.at[d, s, q], recv_sem=gr_sem.at[d, s, q],
            device_id={"hid": towards[d]},
        )

    def hidden_arrival(s, d, q):
        chunk = lax.rem(p + n - 1 - s, n) if d == 0 else lax.rem(p + 1 + s, n)
        block = hidden.at[chunk, pl.ds(d * side + q * piece, piece), :]
        return pltpu.make_async_remote_copy(
            src_ref=block, dst_ref=block,
            send_sem=gs_sem.at[d, s, q], recv_sem=gr_sem.at[d, s, q],
            device_id={"hid": towards[d]},
        )

    for q in range(PIECES):
        for d in range(2):
            sum_copy(n - 2, d, q)[1].wait_recv()
            here = pl.ds(d * side + q * piece, piece)
            there = pl.ds(q * piece, piece)
            scale = rowinv[d * side + q * piece : d * side + (q + 1) * piece, 0:1]
            gate, up = [
                (
                    part[p, here, i * units : (i + 1) * units].astype(F32)
                    + recv[d, n - 2, there, i * units : (i + 1) * units].astype(F32)
                )
                * scale
                for i in range(2)
            ]
            hidden[p, here, :] = (gate / (1.0 + jnp.exp(-gate)) * up).astype(BF16)
            hidden_copy(0, d, q).start()

    for c in range(n):
        down_copy(c).wait()

    width = acc.shape[1]

    def expand(chunk, first, count, fresh):
        here = pl.ds(first, count)
        weights = pl.ds(pl.multiple_of(chunk * units, 128), units)

        def tile(t, _):
            columns = pl.ds(pl.multiple_of(t * TILE, TILE), TILE)
            term = jnp.dot(
                hidden[chunk, here, :], down[weights, columns], preferred_element_type=F32
            )
            acc[here, columns] = term if fresh else acc[here, columns] + term
            return 0

        lax.fori_loop(0, width // TILE, tile, 0)

    expand(p, 0, 2 * side, True)

    def gather(s, _):
        for q in range(PIECES):
            for d in range(2):
                hidden_arrival(s - 1, d, q).wait_recv()

                @pl.when(s < n - 1)
                def _():
                    hidden_copy(s, d, q).start()

        expand(lax.rem(p + n - s, n), 0, side, False)
        expand(lax.rem(p + s, n), side, side, False)
        return 0

    lax.fori_loop(1, n, gather, 0)

    def y_copy(i):
        return pltpu.make_async_remote_copy(
            src_ref=yout.at[i], dst_ref=yin.at[i],
            send_sem=ys_sem.at[i], recv_sem=yr_sem.at[i],
            device_id={"ffn": lax.rem(f + i, m)},
        )

    for i in range(1, m):
        theirs = pl.ds(pl.multiple_of(lax.rem(f + i, m) * rows, rows), rows)
        yout[i] = acc[theirs, :].astype(BF16)
        y_copy(i).start()
    result = tokens_ref[...].astype(F32) + acc[own_rows, :]
    for i in range(1, m):
        y_copy(i).wait_recv()
        result = result + yin[i].astype(F32)
    out_ref[...] = result.astype(BF16)

    for i in range(1, m):
        y_copy(i).wait_send()
        x_copy(i, f).wait_send()
        inverse_copy(i, f).wait_send()
    for i in range(1, n):
        square_copy(i).wait_send()

    def settle(s, _):
        for q in range(PIECES):
            for d in range(2):
                sum_copy(s, d, q)[1].wait_send()
                hidden_copy(s, d, q).wait_send()
        return 0

    lax.fori_loop(0, n - 1, settle, 0)


def ring(n, m, tokens, lang_ids, gain_table, gate_weight, up_weight, down_weight):
    rows, features = tokens.shape
    units = gate_weight.shape[1] // n
    width = down_weight.shape[1]
    count = rows * m
    side = count // 2
    dma = pltpu.SemaphoreType.DMA
    vmem = pl.BlockSpec(memory_space=pltpu.VMEM)
    hbm = pl.BlockSpec(memory_space=pl.ANY)
    return pl.pallas_call(
        functools.partial(kernel, n, m),
        out_shape=jax.ShapeDtypeStruct((rows, width), BF16),
        in_specs=[vmem, vmem, vmem, hbm, hbm, hbm],
        out_specs=vmem,
        scratch_shapes=[
            pltpu.VMEM((count, features), BF16),
            pltpu.VMEM((4, features, 2 * units), BF16),
            pltpu.VMEM((n, count, 2 * units), BF16),
            pltpu.VMEM((2, n - 1, side, 2 * units), BF16),
            pltpu.VMEM((n, count, units), BF16),
            pltpu.VMEM((n * units, width), BF16),
            pltpu.VMEM((count, width), F32),
            pltpu.VMEM((count, 128), F32),
            pltpu.VMEM((n, 8, 128), F32),
            pltpu.VMEM((m, 8, 128), F32),
            pltpu.VMEM((m, rows, width), BF16),
            pltpu.VMEM((m, rows, width), BF16),
            dma((m,)), dma((m,)),
            dma((4, 2)), dma((n,)),
            dma((2, n - 1, PIECES)), dma((2, n - 1, PIECES)),
            dma((2, n - 1, PIECES)), dma((2, n - 1, PIECES)),
            dma((n,)), dma((n,)),
            dma((m,)), dma((m,)),
            dma((m,)), dma((m,)),
        ],
        compiler_params=pltpu.CompilerParams(
            collective_id=0, has_side_effects=True, vmem_limit_bytes=60 * 2**20
        ),
        cost_estimate=pl.CostEstimate(
            flops=6 * count * features * n * units,
            bytes_accessed=6 * features * n * units,
            transcendentals=count * units,
        ),
    )(tokens, lang_ids[:, None], gain_table, gate_weight, up_weight, down_weight)


def solution(mesh):
    n, m = mesh.shape["hid"], mesh.shape["ffn"]

    def local(tokens, lang_ids, gain_table, gate_weight, up_weight, down_weight):
        rows, features = tokens.shape
        unit_count = gate_weight.shape[1]
        fits = (
            n % 2 == 0 and n >= 6 and m >= 2 and rows <= 128
            and unit_count % (n * 128) == 0
            and rows * m % (2 * PIECES * 16) == 0 and rows % 16 == 0
            and down_weight.shape[1] % TILE == 0 and features % 128 == 0
        )
        form = functools.partial(ring, n, m) if fits else gather_then_sum
        return form(tokens, lang_ids, gain_table, gate_weight, up_weight, down_weight)

    return jax.shard_map(
        local,
        mesh=mesh,
        in_specs=(
            P("ffn", "hid"),
            P("ffn"),
            P(None, "hid"),
            P("hid", "ffn"),
            P("hid", "ffn"),
            P("ffn", "hid"),
        ),
        out_specs=P("ffn", "hid"),
        check_vma=False,
    )
```

```python
import functools

import jax
import jax.numpy as jnp
from jax import lax
from jax.experimental import pallas as pl
from jax.experimental.pallas import tpu as pltpu
from jax.sharding import PartitionSpec as P

BF16, F32 = jnp.bfloat16, jnp.float32
PIECES = 4
TILE = 256


def gather_then_sum(tokens, lang_ids, gain_table, gate_weight, up_weight, down_weight):
    hid_count = lax.axis_size("hid")
    unit_count = gate_weight.shape[1]
    feature_total = tokens.shape[1] * hid_count
    one_hot = (
        lang_ids[:, None] == jnp.arange(gain_table.shape[0], dtype=jnp.int32)[None, :]
    ).astype(F32)
    token_gains = jnp.dot(one_hot, gain_table, precision=lax.Precision.HIGHEST)
    values = tokens.astype(F32)
    scaled = (values * token_gains).astype(BF16)
    squares = jnp.sum(values * values, axis=1)
    square_pieces = lax.all_gather(squares, "ffn", axis=0, tiled=True)
    all_squares = lax.psum(square_pieces, "hid")
    inverse_rms = lax.rsqrt(all_squares / feature_total + 1e-05)
    both_weights = jnp.concatenate([gate_weight, up_weight], axis=1)
    gathered = lax.all_gather(scaled, "ffn", axis=0, tiled=True)
    partial_sums = jnp.dot(gathered, both_weights, preferred_element_type=F32)
    summed = lax.psum(partial_sums.astype(BF16), "hid").astype(F32)
    gate_sum = summed[:, :unit_count] * inverse_rms[:, None]
    up_sum = summed[:, unit_count:] * inverse_rms[:, None]
    hidden = (jax.nn.silu(gate_sum) * up_sum).astype(BF16)
    down_terms = jnp.dot(hidden, down_weight, preferred_element_type=F32)
    own_rows = lax.psum_scatter(
        down_terms.astype(BF16), "ffn", scatter_dimension=0, tiled=True
    ).astype(F32)
    return (values + own_rows).astype(BF16)


def kernel(
    n, m, tokens_ref, ids_ref, gain_ref, gate_ref, up_ref, down_ref, out_ref,
    xall, wbuf, part, recv, hidden, down, acc, rowinv, squares, inverse, yout, yin,
    xs_sem, xr_sem, w_sem, d_sem, rs_sem, rr_sem, gs_sem, gr_sem,
    qs_sem, qr_sem, is_sem, ir_sem, ys_sem, yr_sem,
):
    h = lax.axis_index("hid")
    f = lax.axis_index("ffn")
    rows, features = tokens_ref.shape
    units = hidden.shape[2]
    half = n // 2
    side = rows * m // 2
    piece = side // PIECES

    odd = lax.rem(h, 2)
    p = (1 - odd) * (h // 2) + odd * (n - (h + 1) // 2)

    def hid_at(q):
        back = q // half
        return (1 - back) * 2 * q + back * (2 * n - 1 - 2 * q)

    right = hid_at(lax.rem(p + 1, n))
    left = hid_at(lax.rem(p + n - 1, n))
    towards = (right, left)

    def weight_copies(s, b):
        offset = n - 1 - s if b == 0 else lax.rem(s + 1, half)
        chunk = lax.rem(p + offset, n)
        slot = 2 * lax.rem(s, 2) + b
        columns = pl.ds(pl.multiple_of(chunk * units, 128), units)
        return [
            pltpu.make_async_copy(
                ref.at[:, columns], wbuf.at[slot, :, pl.ds(i * units, units)], w_sem.at[slot, i]
            )
            for i, ref in enumerate((gate_ref, up_ref))
        ]

    def start_weights(s):
        for b in range(2):
            for copy in weight_copies(s, b):
                copy.start()

    start_weights(0)
    start_weights(1)

    barrier = pltpu.get_barrier_semaphore()
    for i in range(1, n):
        pl.semaphore_signal(barrier, inc=1, device_id={"hid": lax.rem(h + i, n)})
    for i in range(1, m):
        pl.semaphore_signal(barrier, inc=1, device_id={"ffn": lax.rem(f + i, m)})

    values = tokens_ref[...].astype(F32)
    ids = ids_ref[...]
    gains = jnp.zeros((rows, features), F32)
    for lang in range(gain_ref.shape[0]):
        gains = jnp.where(ids == lang, gain_ref[lang : lang + 1, :], gains)
    own_rows = pl.ds(pl.multiple_of(f * rows, rows), rows)
    xall[own_rows, :] = (values * gains).astype(BF16)
    diagonal = lax.broadcasted_iota(jnp.int32, (rows, 128), 0) == lax.broadcasted_iota(
        jnp.int32, (rows, 128), 1
    )
    sums = jnp.sum(values * values, axis=1, keepdims=True)
    in_lanes = jnp.sum(jnp.where(diagonal, sums, 0.0), axis=0, keepdims=True)
    squares[0] = jnp.broadcast_to(in_lanes, (8, 128))

    pl.semaphore_wait(barrier, n - 1 + m - 1)

    mate = f + 1 - 2 * lax.rem(f, 2)

    def x_copy(i, sender, to):
        block = xall.at[pl.ds(pl.multiple_of(sender * rows, rows), rows), :]
        return pltpu.make_async_remote_copy(
            src_ref=block, dst_ref=block, send_sem=xs_sem.at[i], recv_sem=xr_sem.at[i],
            device_id={"ffn": to},
        )

    def chip_copy(j, sender):
        return x_copy(j, sender, lax.rem(f + 2 * j, m))

    def onward_copy(j, sender):
        return x_copy(m // 2 + j, sender, mate)

    def square_copy(i):
        return pltpu.make_async_remote_copy(
            src_ref=squares.at[0], dst_ref=squares.at[i],
            send_sem=qs_sem.at[i], recv_sem=qr_sem.at[i],
            device_id={"hid": lax.rem(h + i, n)},
        )

    def inverse_copy(i, sender):
        return pltpu.make_async_remote_copy(
            src_ref=inverse.at[sender], dst_ref=inverse.at[sender],
            send_sem=is_sem.at[i], recv_sem=ir_sem.at[i],
            device_id={"ffn": lax.rem(f + i, m)},
        )

    for j in range(1, m // 2):
        chip_copy(j, f).start()
    x_copy(0, f, mate).start()
    for i in range(1, n):
        square_copy(i).start()
    for j in range(1, m // 2):
        sender = lax.rem(f + m - 2 * j, m)
        chip_copy(j, sender).wait_recv()
        onward_copy(j, sender).start()
    x_copy(0, mate, mate).wait_recv()
    for j in range(1, m // 2):
        onward_copy(j, lax.rem(mate + m - 2 * j, m)).wait_recv()

    def project(s, b):
        offset = n - 1 - s if b == 0 else lax.rem(s + 1, half)
        chunk = lax.rem(p + offset, n)
        slot = 2 * lax.rem(s, 2) + b
        for copy in weight_copies(s, b):
            copy.wait()

        def tile(t, _):
            columns = pl.ds(pl.multiple_of(t * TILE, TILE), TILE)
            part[chunk, :, columns] = jnp.dot(
                xall[...], wbuf[slot, :, columns], preferred_element_type=F32
            ).astype(BF16)
            return 0

        lax.fori_loop(0, 2 * units // TILE, tile, 0)

    def sum_copy(s, d, q):
        chunk = lax.rem(p + n - 1 - s, n) if d == 0 else lax.rem(p + 1 + s, n)
        return chunk, pltpu.make_async_remote_copy(
            src_ref=part.at[chunk, pl.ds(d * side + q * piece, piece), :],
            dst_ref=recv.at[d, s, pl.ds(q * piece, piece), :],
            send_sem=rs_sem.at[d, s, q], recv_sem=rr_sem.at[d, s, q],
            device_id={"hid": towards[d]},
        )

    def pass_sums(s, between=None):
        for q in range(PIECES):
            for d in range(2):
                chunk, copy = sum_copy(s, d, q)
                sum_copy(s - 1, d, q)[1].wait_recv()
                here = pl.ds(d * side + q * piece, piece)
                part[chunk, here, :] = (
                    part[chunk, here, :].astype(F32)
                    + recv[d, s - 1, pl.ds(q * piece, piece), :].astype(F32)
                ).astype(BF16)
                copy.start()
            if between is not None:
                between(q)

    for d in range(2):
        project(0, d)
        for q in range(PIECES):
            sum_copy(0, d, q)[1].start()
    start_weights(2)
    project(1, 0)
    project(1, 1)
    start_weights(3)

    def early(s, _):
        def between(q):
            if q == 0:
                project(s + 1, 0)
            if q == PIECES // 2:
                project(s + 1, 1)

        pass_sums(s, between)

        @pl.when(s + 3 < half)
        def _():
            start_weights(s + 3)

        return 0

    lax.fori_loop(1, half - 1, early, 0)

    def down_copy(c):
        block = pl.ds(c * units, units)
        return pltpu.make_async_copy(down_ref.at[block, :], down.at[block, :], d_sem.at[c])

    for c in range(n):
        down_copy(c).start()

    for i in range(1, n):
        square_copy(i).wait_recv()
    total = squares[0]
    for i in range(1, n):
        total = total + squares[i]
    inverse[f] = lax.rsqrt(total / (features * n) + 1e-05)
    for i in range(1, m):
        inverse_copy(i, f).start()
    acc[...] = jnp.zeros_like(acc)

    def late(s, _):
        pass_sums(s)
        return 0

    lax.fori_loop(half - 1, n - 1, late, 0)

    for i in range(1, m):
        inverse_copy(i, lax.rem(f + m - i, m)).wait_recv()
    for j in range(m):
        column = jnp.sum(
            jnp.where(diagonal, inverse[j, 0:1, :], 0.0), axis=1, keepdims=True
        )
        rowinv[j * rows : (j + 1) * rows, :] = jnp.broadcast_to(column, (rows, 128))

    def hidden_copy(s, d, q):
        chunk = lax.rem(p + n - s, n) if d == 0 else lax.rem(p + s, n)
        block = hidden.at[chunk, pl.ds(d * side + q * piece, piece), :]
        return pltpu.make_async_remote_copy(
            src_ref=block, dst_ref=block,
            send_sem=gs_sem.at[d, s, q], recv_sem=gr_sem.at[d, s, q],
            device_id={"hid": towards[d]},
        )

    def hidden_arrival(s, d, q):
        chunk = lax.rem(p + n - 1 - s, n) if d == 0 else lax.rem(p + 1 + s, n)
        block = hidden.at[chunk, pl.ds(d * side + q * piece, piece), :]
        return pltpu.make_async_remote_copy(
            src_ref=block, dst_ref=block,
            send_sem=gs_sem.at[d, s, q], recv_sem=gr_sem.at[d, s, q],
            device_id={"hid": towards[d]},
        )

    for q in range(PIECES):
        for d in range(2):
            sum_copy(n - 2, d, q)[1].wait_recv()
            here = pl.ds(d * side + q * piece, piece)
            there = pl.ds(q * piece, piece)
            scale = rowinv[d * side + q * piece : d * side + (q + 1) * piece, 0:1]
            gate, up = [
                (
                    part[p, here, i * units : (i + 1) * units].astype(F32)
                    + recv[d, n - 2, there, i * units : (i + 1) * units].astype(F32)
                )
                * scale
                for i in range(2)
            ]
            hidden[p, here, :] = (gate / (1.0 + jnp.exp(-gate)) * up).astype(BF16)
            hidden_copy(0, d, q).start()

    for c in range(n):
        down_copy(c).wait()

    width = acc.shape[1]

    def expand(chunk, first, count, tiles):
        here = pl.ds(first, count)
        weights = pl.ds(pl.multiple_of(chunk * units, 128), units)
        for t in tiles:
            columns = slice(t * TILE, (t + 1) * TILE)
            acc[here, columns] += jnp.dot(
                hidden[chunk, here, :], down[weights, columns], preferred_element_type=F32
            )

    every = range(width // TILE)

    def behind(s, tiles):
        expand(lax.rem(p + n - s, n), 0, side, tiles)
        expand(lax.rem(p + s, n), side, side, tiles)

    def gather(s, _):
        for q in range(PIECES):
            for d in range(2):
                hidden_arrival(s - 1, d, q).wait_recv()
                hidden_copy(s, d, q).start()
            behind(s - 1, every[q::PIECES])
        return 0

    lax.fori_loop(1, n - 1, gather, 0)
    behind(n - 2, every)

    def y_copy(to, sender):
        return pltpu.make_async_remote_copy(
            src_ref=yout.at[to], dst_ref=yin.at[sender],
            send_sem=ys_sem.at[to], recv_sem=yr_sem.at[sender],
            device_id={"ffn": to},
        )

    for q in range(PIECES):
        for d in range(2):
            hidden_arrival(n - 2, d, q).wait_recv()
        if (q + 1) * piece % rows == 0:
            for d in range(2):
                j = (d * side + q * piece) // rows
                chunk = lax.rem(p + 1, n) if d == 0 else lax.rem(p + n - 1, n)
                expand(chunk, j * rows, rows, every)

                @pl.when(j != f)
                def _():
                    yout[j] = acc[j * rows : (j + 1) * rows, :].astype(BF16)
                    y_copy(j, f).start()

    result = tokens_ref[...].astype(F32) + acc[own_rows, :]
    for i in range(1, m):
        sender = lax.rem(f + i, m)
        y_copy(sender, sender).wait_recv()
        result = result + yin[sender].astype(F32)
    out_ref[...] = result.astype(BF16)

    for i in range(1, m):
        y_copy(lax.rem(f + i, m), f).wait_send()
        inverse_copy(i, f).wait_send()
    for j in range(1, m // 2):
        chip_copy(j, f).wait_send()
        onward_copy(j, lax.rem(f + m - 2 * j, m)).wait_send()
    x_copy(0, f, mate).wait_send()
    for i in range(1, n):
        square_copy(i).wait_send()

    def settle(s, _):
        for q in range(PIECES):
            for d in range(2):
                sum_copy(s, d, q)[1].wait_send()
                hidden_copy(s, d, q).wait_send()
        return 0

    lax.fori_loop(0, n - 1, settle, 0)


def ring(n, m, tokens, lang_ids, gain_table, gate_weight, up_weight, down_weight):
    rows, features = tokens.shape
    units = gate_weight.shape[1] // n
    width = down_weight.shape[1]
    count = rows * m
    side = count // 2
    dma = pltpu.SemaphoreType.DMA
    vmem = pl.BlockSpec(memory_space=pltpu.VMEM)
    hbm = pl.BlockSpec(memory_space=pl.ANY)
    return pl.pallas_call(
        functools.partial(kernel, n, m),
        out_shape=jax.ShapeDtypeStruct((rows, width), BF16),
        in_specs=[vmem, vmem, vmem, hbm, hbm, hbm],
        out_specs=vmem,
        scratch_shapes=[
            pltpu.VMEM((count, features), BF16),
            pltpu.VMEM((4, features, 2 * units), BF16),
            pltpu.VMEM((n, count, 2 * units), BF16),
            pltpu.VMEM((2, n - 1, side, 2 * units), BF16),
            pltpu.VMEM((n, count, units), BF16),
            pltpu.VMEM((n * units, width), BF16),
            pltpu.VMEM((count, width), F32),
            pltpu.VMEM((count, 128), F32),
            pltpu.VMEM((n, 8, 128), F32),
            pltpu.VMEM((m, 8, 128), F32),
            pltpu.VMEM((m, rows, width), BF16),
            pltpu.VMEM((m, rows, width), BF16),
            dma((m,)), dma((m,)),
            dma((4, 2)), dma((n,)),
            dma((2, n - 1, PIECES)), dma((2, n - 1, PIECES)),
            dma((2, n - 1, PIECES)), dma((2, n - 1, PIECES)),
            dma((n,)), dma((n,)),
            dma((m,)), dma((m,)),
            dma((m,)), dma((m,)),
        ],
        compiler_params=pltpu.CompilerParams(
            collective_id=0, has_side_effects=True, vmem_limit_bytes=60 * 2**20
        ),
        cost_estimate=pl.CostEstimate(
            flops=6 * count * features * n * units,
            bytes_accessed=6 * features * n * units,
            transcendentals=count * units,
        ),
    )(tokens, lang_ids[:, None], gain_table, gate_weight, up_weight, down_weight)


def solution(mesh):
    n, m = mesh.shape["hid"], mesh.shape["ffn"]

    def local(tokens, lang_ids, gain_table, gate_weight, up_weight, down_weight):
        rows, features = tokens.shape
        unit_count = gate_weight.shape[1]
        fits = (
            n % 2 == 0 and n >= 8 and m % 2 == 0 and m >= 4 and rows <= 128
            and unit_count % (n * 128) == 0
            and rows * m % (2 * PIECES * 16) == 0 and rows % 16 == 0
            and rows % (rows * m // (2 * PIECES)) == 0
            and down_weight.shape[1] % TILE == 0 and features % 128 == 0
        )
        form = functools.partial(ring, n, m) if fits else gather_then_sum
        return form(tokens, lang_ids, gain_table, gate_weight, up_weight, down_weight)

    return jax.shard_map(
        local,
        mesh=mesh,
        in_specs=(
            P("ffn", "hid"),
            P("ffn"),
            P(None, "hid"),
            P("hid", "ffn"),
            P("hid", "ffn"),
            P("ffn", "hid"),
        ),
        out_specs=P("ffn", "hid"),
        check_vma=False,
    )
```

```python
import functools

import jax
import jax.numpy as jnp
from jax import lax
from jax.experimental import pallas as pl
from jax.experimental.pallas import tpu as pltpu
from jax.sharding import PartitionSpec as P

BF16, F32 = jnp.bfloat16, jnp.float32
PIECES = 4
TILE = 256


def gather_then_sum(tokens, lang_ids, gain_table, gate_weight, up_weight, down_weight):
    hid_count = lax.axis_size("hid")
    unit_count = gate_weight.shape[1]
    feature_total = tokens.shape[1] * hid_count
    one_hot = (
        lang_ids[:, None] == jnp.arange(gain_table.shape[0], dtype=jnp.int32)[None, :]
    ).astype(F32)
    token_gains = jnp.dot(one_hot, gain_table, precision=lax.Precision.HIGHEST)
    values = tokens.astype(F32)
    scaled = (values * token_gains).astype(BF16)
    squares = jnp.sum(values * values, axis=1)
    square_pieces = lax.all_gather(squares, "ffn", axis=0, tiled=True)
    all_squares = lax.psum(square_pieces, "hid")
    inverse_rms = lax.rsqrt(all_squares / feature_total + 1e-05)
    both_weights = jnp.concatenate([gate_weight, up_weight], axis=1)
    gathered = lax.all_gather(scaled, "ffn", axis=0, tiled=True)
    partial_sums = jnp.dot(gathered, both_weights, preferred_element_type=F32)
    summed = lax.psum(partial_sums.astype(BF16), "hid").astype(F32)
    gate_sum = summed[:, :unit_count] * inverse_rms[:, None]
    up_sum = summed[:, unit_count:] * inverse_rms[:, None]
    hidden = (jax.nn.silu(gate_sum) * up_sum).astype(BF16)
    down_terms = jnp.dot(hidden, down_weight, preferred_element_type=F32)
    own_rows = lax.psum_scatter(
        down_terms.astype(BF16), "ffn", scatter_dimension=0, tiled=True
    ).astype(F32)
    return (values + own_rows).astype(BF16)


def kernel(
    n, m, tokens_ref, ids_ref, gain_ref, gate_ref, up_ref, down_ref, out_ref,
    xall, wbuf, part, recv, hidden, down, acc, rowinv, squares, inverse, yout, yin,
    xs_sem, xr_sem, w_sem, d_sem, rs_sem, rr_sem, gs_sem, gr_sem,
    qs_sem, qr_sem, is_sem, ir_sem, ys_sem, yr_sem,
):
    h = lax.axis_index("hid")
    f = lax.axis_index("ffn")
    rows, features = tokens_ref.shape
    units = hidden.shape[2]
    half = n // 2
    side = rows * m // 2
    piece = side // PIECES

    odd = lax.rem(h, 2)
    p = (1 - odd) * (h // 2) + odd * (n - (h + 1) // 2)

    def hid_at(q):
        back = q // half
        return (1 - back) * 2 * q + back * (2 * n - 1 - 2 * q)

    right = hid_at(lax.rem(p + 1, n))
    left = hid_at(lax.rem(p + n - 1, n))
    towards = (right, left)

    def weight_copies(s, b):
        offset = n - 1 - s if b == 0 else lax.rem(s + 1, half)
        chunk = lax.rem(p + offset, n)
        slot = 2 * lax.rem(s, 2) + b
        columns = pl.ds(pl.multiple_of(chunk * units, 128), units)
        return [
            pltpu.make_async_copy(
                ref.at[:, columns], wbuf.at[slot, :, pl.ds(i * units, units)], w_sem.at[slot, i]
            )
            for i, ref in enumerate((gate_ref, up_ref))
        ]

    def start_weights(s):
        for b in range(2):
            for copy in weight_copies(s, b):
                copy.start()

    start_weights(0)
    start_weights(1)

    barrier = pltpu.get_barrier_semaphore()
    for i in range(1, n):
        pl.semaphore_signal(barrier, inc=1, device_id={"hid": lax.rem(h + i, n)})
    for i in range(1, m):
        pl.semaphore_signal(barrier, inc=1, device_id={"ffn": lax.rem(f + i, m)})

    values = tokens_ref[...].astype(F32)
    turned = lax.broadcasted_iota(jnp.int32, (rows, rows), 0) == lax.broadcasted_iota(
        jnp.int32, (rows, rows), 1
    )
    in_row = jnp.broadcast_to(ids_ref[...].reshape(1, rows).astype(F32), (rows, rows))
    ids = jnp.sum(jnp.where(turned, in_row, 0.0), axis=1, keepdims=True)
    gains = jnp.zeros((rows, features), F32)
    for lang in range(gain_ref.shape[0]):
        gains = jnp.where(ids == float(lang), gain_ref[lang : lang + 1, :], gains)
    own_rows = pl.ds(pl.multiple_of(f * rows, rows), rows)
    xall[own_rows, :] = (values * gains).astype(BF16)
    diagonal = lax.broadcasted_iota(jnp.int32, (rows, 128), 0) == lax.broadcasted_iota(
        jnp.int32, (rows, 128), 1
    )
    sums = jnp.sum(values * values, axis=1, keepdims=True)
    in_lanes = jnp.sum(jnp.where(diagonal, sums, 0.0), axis=0, keepdims=True)
    squares[0] = jnp.broadcast_to(in_lanes, (8, 128))

    pl.semaphore_wait(barrier, n - 1 + m - 1)

    mate = f + 1 - 2 * lax.rem(f, 2)

    def x_copy(i, sender, to):
        block = xall.at[pl.ds(pl.multiple_of(sender * rows, rows), rows), :]
        return pltpu.make_async_remote_copy(
            src_ref=block, dst_ref=block, send_sem=xs_sem.at[i], recv_sem=xr_sem.at[i],
            device_id={"ffn": to},
        )

    def chip_copy(j, sender):
        return x_copy(j, sender, lax.rem(f + 2 * j, m))

    def onward_copy(j, sender):
        return x_copy(m // 2 + j, sender, mate)

    def square_copy(i):
        return pltpu.make_async_remote_copy(
            src_ref=squares.at[0], dst_ref=squares.at[i],
            send_sem=qs_sem.at[i], recv_sem=qr_sem.at[i],
            device_id={"hid": lax.rem(h + i, n)},
        )

    def inverse_copy(i, sender):
        return pltpu.make_async_remote_copy(
            src_ref=inverse.at[sender], dst_ref=inverse.at[sender],
            send_sem=is_sem.at[i], recv_sem=ir_sem.at[i],
            device_id={"ffn": lax.rem(f + i, m)},
        )

    for j in range(1, m // 2):
        chip_copy(j, f).start()
    x_copy(0, f, mate).start()
    for i in range(1, n):
        square_copy(i).start()
    for j in range(1, m // 2):
        sender = lax.rem(f + m - 2 * j, m)
        chip_copy(j, sender).wait_recv()
        onward_copy(j, sender).start()
    x_copy(0, mate, mate).wait_recv()
    for j in range(1, m // 2):
        onward_copy(j, lax.rem(mate + m - 2 * j, m)).wait_recv()

    def project(s, b, first=0, count=2 * side, fetched=False):
        offset = n - 1 - s if b == 0 else lax.rem(s + 1, half)
        chunk = lax.rem(p + offset, n)
        slot = 2 * lax.rem(s, 2) + b
        if not fetched:
            for copy in weight_copies(s, b):
                copy.wait()
        here = pl.ds(first, count)

        def tile(t, _):
            columns = pl.ds(pl.multiple_of(t * TILE, TILE), TILE)
            part[chunk, here, columns] = jnp.dot(
                xall[here, :], wbuf[slot, :, columns], preferred_element_type=F32
            ).astype(BF16)
            return 0

        lax.fori_loop(0, 2 * units // TILE, tile, 0)

    def sum_copy(s, d, q):
        chunk = lax.rem(p + n - 1 - s, n) if d == 0 else lax.rem(p + 1 + s, n)
        return chunk, pltpu.make_async_remote_copy(
            src_ref=part.at[chunk, pl.ds(d * side + q * piece, piece), :],
            dst_ref=recv.at[d, s, pl.ds(q * piece, piece), :],
            send_sem=rs_sem.at[d, s, q], recv_sem=rr_sem.at[d, s, q],
            device_id={"hid": towards[d]},
        )

    def pass_sums(s, between=None):
        for q in range(PIECES):
            for d in range(2):
                chunk, copy = sum_copy(s, d, q)
                sum_copy(s - 1, d, q)[1].wait_recv()
                here = pl.ds(d * side + q * piece, piece)
                part[chunk, here, :] = (
                    part[chunk, here, :].astype(F32)
                    + recv[d, s - 1, pl.ds(q * piece, piece), :].astype(F32)
                ).astype(BF16)
                copy.start()
            if between is not None:
                between(q)

    for d in range(2):
        project(0, d, d * side, side)
        for q in range(PIECES):
            sum_copy(0, d, q)[1].start()
    for d in range(2):
        project(0, d, (1 - d) * side, side, True)
    start_weights(2)
    project(1, 0)
    project(1, 1)
    start_weights(3)

    def early(s, _):
        def between(q):
            if q == 0:
                project(s + 1, 0)
            if q == PIECES // 2:
                project(s + 1, 1)

        pass_sums(s, between)

        @pl.when(s + 3 < half)
        def _():
            start_weights(s + 3)

        return 0

    lax.fori_loop(1, half - 1, early, 0)

    def down_copy(c):
        block = pl.ds(c * units, units)
        return pltpu.make_async_copy(down_ref.at[block, :], down.at[block, :], d_sem.at[c])

    for c in range(n):
        down_copy(c).start()

    for i in range(1, n):
        square_copy(i).wait_recv()
    total = squares[0]
    for i in range(1, n):
        total = total + squares[i]
    inverse[f] = lax.rsqrt(total / (features * n) + 1e-05)
    for i in range(1, m):
        inverse_copy(i, f).start()
    acc[...] = jnp.zeros_like(acc)

    def late(s, _):
        pass_sums(s)
        return 0

    lax.fori_loop(half - 1, n - 1, late, 0)

    for i in range(1, m):
        inverse_copy(i, lax.rem(f + m - i, m)).wait_recv()
    for j in range(m):
        column = jnp.sum(
            jnp.where(diagonal, inverse[j, 0:1, :], 0.0), axis=1, keepdims=True
        )
        rowinv[j * rows : (j + 1) * rows, :] = jnp.broadcast_to(column, (rows, 128))

    def hidden_copy(s, d, q):
        chunk = lax.rem(p + n - s, n) if d == 0 else lax.rem(p + s, n)
        block = hidden.at[chunk, pl.ds(d * side + q * piece, piece), :]
        return pltpu.make_async_remote_copy(
            src_ref=block, dst_ref=block,
            send_sem=gs_sem.at[d, s, q], recv_sem=gr_sem.at[d, s, q],
            device_id={"hid": towards[d]},
        )

    def hidden_arrival(s, d, q):
        chunk = lax.rem(p + n - 1 - s, n) if d == 0 else lax.rem(p + 1 + s, n)
        block = hidden.at[chunk, pl.ds(d * side + q * piece, piece), :]
        return pltpu.make_async_remote_copy(
            src_ref=block, dst_ref=block,
            send_sem=gs_sem.at[d, s, q], recv_sem=gr_sem.at[d, s, q],
            device_id={"hid": towards[d]},
        )

    for q in range(PIECES):
        for d in range(2):
            sum_copy(n - 2, d, q)[1].wait_recv()
            here = pl.ds(d * side + q * piece, piece)
            there = pl.ds(q * piece, piece)
            scale = rowinv[d * side + q * piece : d * side + (q + 1) * piece, 0:1]
            gate, up = [
                (
                    part[p, here, i * units : (i + 1) * units].astype(F32)
                    + recv[d, n - 2, there, i * units : (i + 1) * units].astype(F32)
                )
                * scale
                for i in range(2)
            ]
            hidden[p, here, :] = (gate / (1.0 + jnp.exp(-gate)) * up).astype(BF16)
            hidden_copy(0, d, q).start()

    for c in range(n):
        down_copy(c).wait()

    width = acc.shape[1]

    def expand(chunk, first, count, tiles):
        here = pl.ds(first, count)
        weights = pl.ds(pl.multiple_of(chunk * units, 128), units)
        for t in tiles:
            columns = slice(t * TILE, (t + 1) * TILE)
            acc[here, columns] += jnp.dot(
                hidden[chunk, here, :], down[weights, columns], preferred_element_type=F32
            )

    every = range(width // TILE)

    def behind(s, tiles):
        expand(lax.rem(p + n - s, n), 0, side, tiles)
        expand(lax.rem(p + s, n), side, side, tiles)

    def gather(s, _):
        for q in range(PIECES):
            for d in range(2):
                hidden_arrival(s - 1, d, q).wait_recv()
                hidden_copy(s, d, q).start()
            behind(s - 1, every[q::PIECES])
        return 0

    lax.fori_loop(1, n - 1, gather, 0)
    behind(n - 2, every)

    def y_copy(to, sender):
        return pltpu.make_async_remote_copy(
            src_ref=yout.at[to], dst_ref=yin.at[sender],
            send_sem=ys_sem.at[to], recv_sem=yr_sem.at[sender],
            device_id={"ffn": to},
        )

    for q in range(PIECES):
        for d in range(2):
            hidden_arrival(n - 2, d, q).wait_recv()
        if (q + 1) * piece % rows == 0:
            for away in range(2):
                d = lax.rem(2 * f // m + 1 + away, 2)
                j = d * (m // 2) + q * piece // rows
                chunk = lax.rem(p + 1 + d * (n - 2), n)
                there = pl.ds(pl.multiple_of(j * rows, rows), rows)
                expand(chunk, pl.multiple_of(j * rows, rows), rows, every)

                @pl.when(j != f)
                def _():
                    yout[j] = acc[there, :].astype(BF16)
                    y_copy(j, f).start()

    result = tokens_ref[...].astype(F32) + acc[own_rows, :]
    for i in range(1, m):
        sender = lax.rem(f + i, m)
        y_copy(sender, sender).wait_recv()
        result = result + yin[sender].astype(F32)
    out_ref[...] = result.astype(BF16)

    for i in range(1, m):
        y_copy(lax.rem(f + i, m), f).wait_send()
        inverse_copy(i, f).wait_send()
    for j in range(1, m // 2):
        chip_copy(j, f).wait_send()
        onward_copy(j, lax.rem(f + m - 2 * j, m)).wait_send()
    x_copy(0, f, mate).wait_send()
    for i in range(1, n):
        square_copy(i).wait_send()

    def settle(s, _):
        for q in range(PIECES):
            for d in range(2):
                sum_copy(s, d, q)[1].wait_send()
                hidden_copy(s, d, q).wait_send()
        return 0

    lax.fori_loop(0, n - 1, settle, 0)


def ring(n, m, tokens, lang_ids, gain_table, gate_weight, up_weight, down_weight):
    rows, features = tokens.shape
    units = gate_weight.shape[1] // n
    width = down_weight.shape[1]
    count = rows * m
    side = count // 2
    dma = pltpu.SemaphoreType.DMA
    vmem = pl.BlockSpec(memory_space=pltpu.VMEM)
    hbm = pl.BlockSpec(memory_space=pl.ANY)
    return pl.pallas_call(
        functools.partial(kernel, n, m),
        out_shape=jax.ShapeDtypeStruct((rows, width), BF16),
        in_specs=[vmem, vmem, vmem, hbm, hbm, hbm],
        out_specs=vmem,
        scratch_shapes=[
            pltpu.VMEM((count, features), BF16),
            pltpu.VMEM((4, features, 2 * units), BF16),
            pltpu.VMEM((n, count, 2 * units), BF16),
            pltpu.VMEM((2, n - 1, side, 2 * units), BF16),
            pltpu.VMEM((n, count, units), BF16),
            pltpu.VMEM((n * units, width), BF16),
            pltpu.VMEM((count, width), F32),
            pltpu.VMEM((count, 128), F32),
            pltpu.VMEM((n, 8, 128), F32),
            pltpu.VMEM((m, 8, 128), F32),
            pltpu.VMEM((m, rows, width), BF16),
            pltpu.VMEM((m, rows, width), BF16),
            dma((m,)), dma((m,)),
            dma((4, 2)), dma((n,)),
            dma((2, n - 1, PIECES)), dma((2, n - 1, PIECES)),
            dma((2, n - 1, PIECES)), dma((2, n - 1, PIECES)),
            dma((n,)), dma((n,)),
            dma((m,)), dma((m,)),
            dma((m,)), dma((m,)),
        ],
        compiler_params=pltpu.CompilerParams(
            collective_id=0, has_side_effects=True, vmem_limit_bytes=60 * 2**20
        ),
        cost_estimate=pl.CostEstimate(
            flops=6 * count * features * n * units,
            bytes_accessed=6 * features * n * units,
            transcendentals=count * units,
        ),
    )(tokens, lang_ids, gain_table, gate_weight, up_weight, down_weight)


def solution(mesh):
    n, m = mesh.shape["hid"], mesh.shape["ffn"]

    def local(tokens, lang_ids, gain_table, gate_weight, up_weight, down_weight):
        rows, features = tokens.shape
        unit_count = gate_weight.shape[1]
        fits = (
            n % 2 == 0 and n >= 8 and m % 2 == 0 and m >= 4 and rows <= 128
            and unit_count % (n * 128) == 0
            and rows * m % (2 * PIECES * 16) == 0 and rows % 16 == 0
            and rows % (rows * m // (2 * PIECES)) == 0
            and down_weight.shape[1] % TILE == 0 and features % 128 == 0
        )
        form = functools.partial(ring, n, m) if fits else gather_then_sum
        return form(tokens, lang_ids, gain_table, gate_weight, up_weight, down_weight)

    return jax.shard_map(
        local,
        mesh=mesh,
        in_specs=(
            P("ffn", "hid"),
            P("ffn"),
            P(None, "hid"),
            P("hid", "ffn"),
            P("hid", "ffn"),
            P("ffn", "hid"),
        ),
        out_specs=P("ffn", "hid"),
        check_vma=False,
    )
```

```python
import functools

import jax
import jax.numpy as jnp
from jax import lax
from jax.experimental import pallas as pl
from jax.experimental.pallas import tpu as pltpu
from jax.sharding import PartitionSpec as P

BF16, F32 = jnp.bfloat16, jnp.float32
PIECES = 4
TILE = 256


def gather_then_sum(tokens, lang_ids, gain_table, gate_weight, up_weight, down_weight):
    hid_count = lax.axis_size("hid")
    unit_count = gate_weight.shape[1]
    feature_total = tokens.shape[1] * hid_count
    one_hot = (
        lang_ids[:, None] == jnp.arange(gain_table.shape[0], dtype=jnp.int32)[None, :]
    ).astype(F32)
    token_gains = jnp.dot(one_hot, gain_table, precision=lax.Precision.HIGHEST)
    values = tokens.astype(F32)
    scaled = (values * token_gains).astype(BF16)
    squares = jnp.sum(values * values, axis=1)
    square_pieces = lax.all_gather(squares, "ffn", axis=0, tiled=True)
    all_squares = lax.psum(square_pieces, "hid")
    inverse_rms = lax.rsqrt(all_squares / feature_total + 1e-05)
    both_weights = jnp.concatenate([gate_weight, up_weight], axis=1)
    gathered = lax.all_gather(scaled, "ffn", axis=0, tiled=True)
    partial_sums = jnp.dot(gathered, both_weights, preferred_element_type=F32)
    summed = lax.psum(partial_sums.astype(BF16), "hid").astype(F32)
    gate_sum = summed[:, :unit_count] * inverse_rms[:, None]
    up_sum = summed[:, unit_count:] * inverse_rms[:, None]
    hidden = (jax.nn.silu(gate_sum) * up_sum).astype(BF16)
    down_terms = jnp.dot(hidden, down_weight, preferred_element_type=F32)
    own_rows = lax.psum_scatter(
        down_terms.astype(BF16), "ffn", scatter_dimension=0, tiled=True
    ).astype(F32)
    return (values + own_rows).astype(BF16)


def kernel(
    n, m, tokens_ref, ids_ref, gain_ref, gate_ref, up_ref, down_ref, out_ref,
    xall, wbuf, part, recv, hidden, down, acc, rowinv, squares, inverse, yout, yin,
    xs_sem, xr_sem, w_sem, d_sem, rs_sem, rr_sem, gs_sem, gr_sem,
    qs_sem, qr_sem, is_sem, ir_sem, ys_sem, yr_sem,
):
    h = lax.axis_index("hid")
    f = lax.axis_index("ffn")
    rows, features = tokens_ref.shape
    units = hidden.shape[2]
    half = n // 2
    side = rows * m // 2
    piece = side // PIECES

    odd = lax.rem(h, 2)
    p = (1 - odd) * (h // 2) + odd * (n - (h + 1) // 2)

    def hid_at(q):
        back = q // half
        return (1 - back) * 2 * q + back * (2 * n - 1 - 2 * q)

    right = hid_at(lax.rem(p + 1, n))
    left = hid_at(lax.rem(p + n - 1, n))
    towards = (right, left)

    def weight_copies(s, b):
        offset = n - 1 - s if b == 0 else lax.rem(s + 1, half)
        chunk = lax.rem(p + offset, n)
        slot = 2 * lax.rem(s, 2) + b
        columns = pl.ds(pl.multiple_of(chunk * units, 128), units)
        return [
            pltpu.make_async_copy(
                ref.at[:, columns], wbuf.at[slot, :, pl.ds(i * units, units)], w_sem.at[slot, i]
            )
            for i, ref in enumerate((gate_ref, up_ref))
        ]

    def start_weights(s):
        for b in range(2):
            for copy in weight_copies(s, b):
                copy.start()

    start_weights(0)
    start_weights(1)

    barrier = pltpu.get_barrier_semaphore()
    for i in range(1, n):
        pl.semaphore_signal(barrier, inc=1, device_id={"hid": lax.rem(h + i, n)})
    for i in range(1, m):
        pl.semaphore_signal(barrier, inc=1, device_id={"ffn": lax.rem(f + i, m)})

    values = tokens_ref[...].astype(F32)
    turned = lax.broadcasted_iota(jnp.int32, (rows, rows), 0) == lax.broadcasted_iota(
        jnp.int32, (rows, rows), 1
    )
    in_row = jnp.broadcast_to(ids_ref[...].reshape(1, rows).astype(F32), (rows, rows))
    ids = jnp.sum(jnp.where(turned, in_row, 0.0), axis=1, keepdims=True)
    gains = jnp.zeros((rows, features), F32)
    for lang in range(gain_ref.shape[0]):
        gains = jnp.where(ids == float(lang), gain_ref[lang : lang + 1, :], gains)
    own_rows = pl.ds(pl.multiple_of(f * rows, rows), rows)
    xall[own_rows, :] = (values * gains).astype(BF16)
    diagonal = lax.broadcasted_iota(jnp.int32, (rows, 128), 0) == lax.broadcasted_iota(
        jnp.int32, (rows, 128), 1
    )
    sums = jnp.sum(values * values, axis=1, keepdims=True)
    in_lanes = jnp.sum(jnp.where(diagonal, sums, 0.0), axis=0, keepdims=True)
    squares[0] = jnp.broadcast_to(in_lanes, (8, 128))

    pl.semaphore_wait(barrier, n - 1 + m - 1)

    mate = f + 1 - 2 * lax.rem(f, 2)

    def x_copy(i, sender, to):
        block = xall.at[pl.ds(pl.multiple_of(sender * rows, rows), rows), :]
        return pltpu.make_async_remote_copy(
            src_ref=block, dst_ref=block, send_sem=xs_sem.at[i], recv_sem=xr_sem.at[i],
            device_id={"ffn": to},
        )

    def chip_copy(j, sender):
        return x_copy(j, sender, lax.rem(f + 2 * j, m))

    def onward_copy(j, sender):
        return x_copy(m // 2 + j, sender, mate)

    def square_copy(i):
        return pltpu.make_async_remote_copy(
            src_ref=squares.at[0], dst_ref=squares.at[i],
            send_sem=qs_sem.at[i], recv_sem=qr_sem.at[i],
            device_id={"hid": lax.rem(h + i, n)},
        )

    def inverse_copy(i, sender):
        return pltpu.make_async_remote_copy(
            src_ref=inverse.at[sender], dst_ref=inverse.at[sender],
            send_sem=is_sem.at[i], recv_sem=ir_sem.at[i],
            device_id={"ffn": lax.rem(f + i, m)},
        )

    for j in range(1, m // 2):
        chip_copy(j, f).start()
    x_copy(0, f, mate).start()
    for i in range(1, n):
        square_copy(i).start()
    for j in range(1, m // 2):
        sender = lax.rem(f + m - 2 * j, m)
        chip_copy(j, sender).wait_recv()
        onward_copy(j, sender).start()
    x_copy(0, mate, mate).wait_recv()
    for j in range(1, m // 2):
        onward_copy(j, lax.rem(mate + m - 2 * j, m)).wait_recv()

    def project(s, b, first=0, count=2 * side, fetched=False):
        offset = n - 1 - s if b == 0 else lax.rem(s + 1, half)
        chunk = lax.rem(p + offset, n)
        slot = 2 * lax.rem(s, 2) + b
        if not fetched:
            for copy in weight_copies(s, b):
                copy.wait()
        here = pl.ds(first, count)

        def tile(t, _):
            columns = pl.ds(pl.multiple_of(t * TILE, TILE), TILE)
            part[chunk, here, columns] = jnp.dot(
                xall[here, :], wbuf[slot, :, columns], preferred_element_type=F32
            ).astype(BF16)
            return 0

        lax.fori_loop(0, 2 * units // TILE, tile, 0)

    def sum_copy(s, d, q):
        chunk = lax.rem(p + n - 1 - s, n) if d == 0 else lax.rem(p + 1 + s, n)
        return chunk, pltpu.make_async_remote_copy(
            src_ref=part.at[chunk, pl.ds(d * side + q * piece, piece), :],
            dst_ref=recv.at[d, s, pl.ds(q * piece, piece), :],
            send_sem=rs_sem.at[d, s, q], recv_sem=rr_sem.at[d, s, q],
            device_id={"hid": towards[d]},
        )

    def pass_sums(s, between=None):
        for q in range(PIECES):
            for d in range(2):
                chunk, copy = sum_copy(s, d, q)
                sum_copy(s - 1, d, q)[1].wait_recv()
                here = pl.ds(d * side + q * piece, piece)
                part[chunk, here, :] = (
                    part[chunk, here, :].astype(F32)
                    + recv[d, s - 1, pl.ds(q * piece, piece), :].astype(F32)
                ).astype(BF16)
                copy.start()
            if between is not None:
                between(q)

    for d in range(2):
        project(0, d, d * side, side)
        sum_copy(0, d, 0)[1].start()

    def start_piece(q):
        for d in range(2):
            sum_copy(0, d, q)[1].start()

    project(0, 0, side, side, True)
    start_piece(1)
    project(0, 1, 0, side, True)
    start_weights(2)
    start_piece(2)
    project(1, 0)
    for q in range(3, PIECES):
        start_piece(q)
    project(1, 1)
    start_weights(3)

    def early(s, _):
        def between(q):
            if q == 0:
                project(s + 1, 0)
            if q == PIECES // 2:
                project(s + 1, 1)

        pass_sums(s, between)

        @pl.when(s + 3 < half)
        def _():
            start_weights(s + 3)

        return 0

    lax.fori_loop(1, half - 1, early, 0)

    def down_copy(c):
        block = pl.ds(c * units, units)
        return pltpu.make_async_copy(down_ref.at[block, :], down.at[block, :], d_sem.at[c])

    for c in range(n):
        down_copy(c).start()

    for i in range(1, n):
        square_copy(i).wait_recv()
    total = squares[0]
    for i in range(1, n):
        total = total + squares[i]
    inverse[f] = lax.rsqrt(total / (features * n) + 1e-05)
    for i in range(1, m):
        inverse_copy(i, f).start()
    acc[...] = jnp.zeros_like(acc)

    def late(s, _):
        pass_sums(s)
        return 0

    lax.fori_loop(half - 1, n - 1, late, 0)

    for i in range(1, m):
        inverse_copy(i, lax.rem(f + m - i, m)).wait_recv()
    for j in range(m):
        column = jnp.sum(
            jnp.where(diagonal, inverse[j, 0:1, :], 0.0), axis=1, keepdims=True
        )
        rowinv[j * rows : (j + 1) * rows, :] = jnp.broadcast_to(column, (rows, 128))

    def hidden_copy(s, d, q):
        chunk = lax.rem(p + n - s, n) if d == 0 else lax.rem(p + s, n)
        block = hidden.at[chunk, pl.ds(d * side + q * piece, piece), :]
        return pltpu.make_async_remote_copy(
            src_ref=block, dst_ref=block,
            send_sem=gs_sem.at[d, s, q], recv_sem=gr_sem.at[d, s, q],
            device_id={"hid": towards[d]},
        )

    def hidden_arrival(s, d, q):
        chunk = lax.rem(p + n - 1 - s, n) if d == 0 else lax.rem(p + 1 + s, n)
        block = hidden.at[chunk, pl.ds(d * side + q * piece, piece), :]
        return pltpu.make_async_remote_copy(
            src_ref=block, dst_ref=block,
            send_sem=gs_sem.at[d, s, q], recv_sem=gr_sem.at[d, s, q],
            device_id={"hid": towards[d]},
        )

    for q in range(PIECES):
        for d in range(2):
            sum_copy(n - 2, d, q)[1].wait_recv()
            here = pl.ds(d * side + q * piece, piece)
            there = pl.ds(q * piece, piece)
            scale = rowinv[d * side + q * piece : d * side + (q + 1) * piece, 0:1]
            gate, up = [
                (
                    part[p, here, i * units : (i + 1) * units].astype(F32)
                    + recv[d, n - 2, there, i * units : (i + 1) * units].astype(F32)
                )
                * scale
                for i in range(2)
            ]
            hidden[p, here, :] = (gate / (1.0 + jnp.exp(-gate)) * up).astype(BF16)
            hidden_copy(0, d, q).start()

    for c in range(n):
        down_copy(c).wait()

    width = acc.shape[1]

    def expand(chunk, first, count, tiles):
        here = pl.ds(first, count)
        weights = pl.ds(pl.multiple_of(chunk * units, 128), units)
        for t in tiles:
            columns = slice(t * TILE, (t + 1) * TILE)
            acc[here, columns] += jnp.dot(
                hidden[chunk, here, :], down[weights, columns], preferred_element_type=F32
            )

    every = range(width // TILE)

    def behind(s, tiles):
        expand(lax.rem(p + n - s, n), 0, side, tiles)
        expand(lax.rem(p + s, n), side, side, tiles)

    def gather(s, _):
        for q in range(PIECES):
            for d in range(2):
                hidden_arrival(s - 1, d, q).wait_recv()
                hidden_copy(s, d, q).start()
            behind(s - 1, every[q::PIECES])
        return 0

    lax.fori_loop(1, n - 1, gather, 0)
    behind(n - 2, every)

    def y_copy(to, sender):
        return pltpu.make_async_remote_copy(
            src_ref=yout.at[to], dst_ref=yin.at[sender],
            send_sem=ys_sem.at[to], recv_sem=yr_sem.at[sender],
            device_id={"ffn": to},
        )

    for q in range(PIECES):
        for d in range(2):
            hidden_arrival(n - 2, d, q).wait_recv()
        if (q + 1) * piece % rows == 0:
            for away in range(2):
                d = lax.rem(2 * f // m + 1 + away, 2)
                j = d * (m // 2) + q * piece // rows
                chunk = lax.rem(p + 1 + d * (n - 2), n)
                there = pl.ds(pl.multiple_of(j * rows, rows), rows)
                expand(chunk, pl.multiple_of(j * rows, rows), rows, every)

                @pl.when(j != f)
                def _():
                    yout[j] = acc[there, :].astype(BF16)
                    y_copy(j, f).start()

    result = tokens_ref[...].astype(F32) + acc[own_rows, :]
    for i in range(1, m):
        sender = lax.rem(f + i, m)
        y_copy(sender, sender).wait_recv()
        result = result + yin[sender].astype(F32)
    out_ref[...] = result.astype(BF16)

    for i in range(1, m):
        y_copy(lax.rem(f + i, m), f).wait_send()
        inverse_copy(i, f).wait_send()
    for j in range(1, m // 2):
        chip_copy(j, f).wait_send()
        onward_copy(j, lax.rem(f + m - 2 * j, m)).wait_send()
    x_copy(0, f, mate).wait_send()
    for i in range(1, n):
        square_copy(i).wait_send()

    def settle(s, _):
        for q in range(PIECES):
            for d in range(2):
                sum_copy(s, d, q)[1].wait_send()
                hidden_copy(s, d, q).wait_send()
        return 0

    lax.fori_loop(0, n - 1, settle, 0)


def ring(n, m, tokens, lang_ids, gain_table, gate_weight, up_weight, down_weight):
    rows, features = tokens.shape
    units = gate_weight.shape[1] // n
    width = down_weight.shape[1]
    count = rows * m
    side = count // 2
    dma = pltpu.SemaphoreType.DMA
    vmem = pl.BlockSpec(memory_space=pltpu.VMEM)
    hbm = pl.BlockSpec(memory_space=pl.ANY)
    return pl.pallas_call(
        functools.partial(kernel, n, m),
        out_shape=jax.ShapeDtypeStruct((rows, width), BF16),
        in_specs=[vmem, vmem, vmem, hbm, hbm, hbm],
        out_specs=vmem,
        scratch_shapes=[
            pltpu.VMEM((count, features), BF16),
            pltpu.VMEM((4, features, 2 * units), BF16),
            pltpu.VMEM((n, count, 2 * units), BF16),
            pltpu.VMEM((2, n - 1, side, 2 * units), BF16),
            pltpu.VMEM((n, count, units), BF16),
            pltpu.VMEM((n * units, width), BF16),
            pltpu.VMEM((count, width), F32),
            pltpu.VMEM((count, 128), F32),
            pltpu.VMEM((n, 8, 128), F32),
            pltpu.VMEM((m, 8, 128), F32),
            pltpu.VMEM((m, rows, width), BF16),
            pltpu.VMEM((m, rows, width), BF16),
            dma((m,)), dma((m,)),
            dma((4, 2)), dma((n,)),
            dma((2, n - 1, PIECES)), dma((2, n - 1, PIECES)),
            dma((2, n - 1, PIECES)), dma((2, n - 1, PIECES)),
            dma((n,)), dma((n,)),
            dma((m,)), dma((m,)),
            dma((m,)), dma((m,)),
        ],
        compiler_params=pltpu.CompilerParams(
            collective_id=0, has_side_effects=True, vmem_limit_bytes=60 * 2**20
        ),
        cost_estimate=pl.CostEstimate(
            flops=6 * count * features * n * units,
            bytes_accessed=6 * features * n * units,
            transcendentals=count * units,
        ),
    )(tokens, lang_ids, gain_table, gate_weight, up_weight, down_weight)


def solution(mesh):
    n, m = mesh.shape["hid"], mesh.shape["ffn"]

    def local(tokens, lang_ids, gain_table, gate_weight, up_weight, down_weight):
        rows, features = tokens.shape
        unit_count = gate_weight.shape[1]
        fits = (
            n % 2 == 0 and n >= 8 and m % 2 == 0 and m >= 4 and rows <= 128
            and unit_count % (n * 128) == 0
            and rows * m % (2 * PIECES * 16) == 0 and rows % 16 == 0
            and rows % (rows * m // (2 * PIECES)) == 0
            and down_weight.shape[1] % TILE == 0 and features % 128 == 0
        )
        form = functools.partial(ring, n, m) if fits else gather_then_sum
        return form(tokens, lang_ids, gain_table, gate_weight, up_weight, down_weight)

    return jax.shard_map(
        local,
        mesh=mesh,
        in_specs=(
            P("ffn", "hid"),
            P("ffn"),
            P(None, "hid"),
            P("hid", "ffn"),
            P("hid", "ffn"),
            P("ffn", "hid"),
        ),
        out_specs=P("ffn", "hid"),
        check_vma=False,
    )
```
